128 devices in a mesh: row: 8 (over y, core), col: 16 (over z, x).
Axes of the slice: x: 4, y: 4, z: 4, core: 2. Of those that a mesh axis runs over, the one named last changes fastest.
Arguments:
- tokens: bfloat16 [256, 512, 1024], P('row', 'col'), may hold values from -6 to 6
- ln_gain: float32 [1024], replicated, may hold values from 0.25 to 1.75
- w_query: bfloat16 [1024, 1024], replicated, may hold values from -0.1875 to 0.1875
- w_keyval: bfloat16 [1024, 2048], replicated, may hold values from -0.1875 to 0.1875
- logit_scale: float32 [16], replicated, may hold values from 2 to 40
- w_output: bfloat16 [1024, 1024], replicated, may hold values from -0.75 to 0.75
- parents: int32 [32, 64, 3, 8], P('row', 'col'), may hold values from 0 to 32767, as said below
- child_counts: int32 [32, 64, 3, 8], P('row', 'col'), may hold values from 1 to 4
Outputs:
- mixed: bfloat16 [256, 512, 1024], P('row', 'col')
The draws below stay inside these ranges and needn't reach their ends.
Inputs may be any that keep to these rules, and one draw needn't show every extreme that they name: `parents`: every entry names a cell of its level's grid as in the reference program. The 8 entries of one tile and level are distinct, and so are all entries of one level over the tiles of one device. Over the tiles of one device and one level at most 2 entries name cells in the block of one device, and in every draw some device receives exactly 2 from some device at every level.
All inputs are finite; a program needn't handle non-finite values.
Results may differ from the reference program's by a relative error of at most 0.012.
The reference program's roundings to bfloat16 on the way count: a program that leaves them out, or rounds other values in their place, can miss the bound.
Values may be sent and summed in bfloat16 or wider, within the bound.
A program may use at most 128 MiB of HBM per device.

```python
import math
import jax
import jax.numpy as jnp
from jax import lax

D = 1024
HEADS = 16
ROWS_DEV = 32
COLS_DEV = 32
TILE = 8
LEVELS = 3
TOPK = 8
NR = 256
NC = 512
N_ROW = 8
N_COL = 16
DEVICES = 128


def draw_parents(key, part):
    key = jax.random.fold_in(key, 7)
    tiles_rows = ROWS_DEV // TILE
    tiles_cols = COLS_DEV // TILE
    requests = tiles_rows * tiles_cols * TOPK
    multiple = max(1, requests // DEVICES)
    most_doubled = min(requests, DEVICES) // 2
    level_cells = jnp.array([(ROWS_DEV >> level_no + 1) * (COLS_DEV >> level_no + 1) for level_no in range(LEVELS)], jnp.int32)

    def one_block(block_key, cell_count):
        sub_keys = jax.random.split(block_key, 5)
        doubled = jax.random.randint(sub_keys[0], (), 1, most_doubled + 1)
        labels = jax.random.permutation(sub_keys[1], DEVICES)
        request_no = jnp.arange(requests, dtype=jnp.int32)
        column = request_no % DEVICES
        shifted = (column >= doubled) & (column < 2 * doubled)
        target = jnp.where(shifted, column - doubled, column)
        slot_rank = request_no // DEVICES + jnp.where(shifted, multiple, 0)
        first_cell = jax.random.randint(sub_keys[2], (DEVICES,), 0, cell_count)
        stride = 2 * jax.random.randint(sub_keys[3], (DEVICES,), 0, jnp.maximum(cell_count // 2, 1)) + 1
        local_cell = (first_cell[target] + slot_rank * stride[target]) % cell_count
        chosen = labels[target] * cell_count + local_cell
        return chosen[jax.random.permutation(sub_keys[4], requests)]
    block_keys = jax.random.split(key, DEVICES * LEVELS)
    cells_all = jnp.tile(level_cells, DEVICES)
    drawn = jax.vmap(one_block)(block_keys, cells_all)
    drawn = drawn.reshape(N_ROW, N_COL, LEVELS, tiles_rows, tiles_cols, TOPK)
    drawn = drawn.transpose(0, 3, 1, 4, 2, 5)
    return drawn.reshape(N_ROW * tiles_rows, N_COL * tiles_cols, LEVELS, TOPK).astype(jnp.int32)


def set_ends(values, key, least, largest):
    longest = values.shape.index(max(values.shape))
    spots = []
    for shift in (0, 1):
        where = [jax.random.randint(jax.random.fold_in(key, axis), (), 0, length) for axis, length in enumerate(values.shape)]
        where[longest] = (where[longest] + shift) % values.shape[longest]
        spots.append(tuple(where))
    return values.at[spots[0]].set(least).at[spots[1]].set(largest)


def block_levels(stream_key, shape, cuts, low, largest):
    factor_of, own = 1.0, jax.random.fold_in(stream_key, 6)
    for axis_at, blocks in cuts:
        steps = jnp.exp(jax.random.uniform(jax.random.fold_in(own, axis_at), (blocks,), jnp.float32, low / len(cuts), largest / len(cuts)))
        factor_of = factor_of * jnp.repeat(steps, shape[axis_at] // blocks).reshape([-1 if axis == axis_at else 1 for axis in range(len(shape))])
    return factor_of


def bell_draw(stream_key, extent, deviation, reach, cuts=(), kind=jnp.bfloat16):
    level = block_levels(stream_key, extent, cuts, -0.22, 0.18) if cuts else 1.0
    values = jax.random.normal(stream_key, extent, jnp.float32) * deviation * level
    return jnp.minimum(jnp.maximum(values, -reach), reach).astype(kind)


def setup_inputs(seed: int = 0) -> dict:
    key_of = jax.random.split(jax.random.key(seed), 9)
    tokens = bell_draw(key_of[0], (NR, NC, D), 1.0, 6.0, ((0, 8), (1, 16)))
    ln_gain = jnp.clip(1.0 + 0.15 * jax.random.normal(key_of[1], (D,), jnp.float32), 0.25, 1.75)
    w_query = bell_draw(key_of[2], (D, D), D ** -0.5, 0.1875)
    w_keyval = bell_draw(key_of[3], (D, 2 * D), D ** -0.5, 0.1875)
    logit_scale = jnp.clip(jnp.exp(jax.random.uniform(key_of[4], (HEADS,), jnp.float32, math.log(2.0), math.log(40.0))), 2.0, 40.0)
    w_output = bell_draw(key_of[5], (D, D), (D // 16) ** -0.5, 0.75)
    parents = draw_parents(jax.random.fold_in(key_of[8], 71), 0)
    child_counts = set_ends(jax.random.randint(key_of[7], (NR // TILE, NC // TILE, LEVELS, TOPK), 1, 5), jax.random.fold_in(key_of[7], 1), 1, 4).astype(jnp.int32)
    return {"tokens": tokens, "ln_gain": ln_gain, "w_query": w_query, "w_keyval": w_keyval, "logit_scale": logit_scale, "w_output": w_output, "parents": parents, "child_counts": child_counts}


EPSILON = 1e-06

def layer_norm(flat, gain):
    centre = lax.optimization_barrier(jnp.mean(flat, axis=-1, keepdims=True))
    centered = flat - centre
    spread = lax.optimization_barrier(jnp.mean(centered * centered, axis=-1, keepdims=True))
    return centered * lax.rsqrt(spread + EPSILON) * gain

def normalize_heads(values, scale_row, head_count):
    shaped = values.reshape(values.shape[:-1] + (head_count, values.shape[-1] // head_count))
    squares = lax.optimization_barrier(jnp.sum(shaped * shaped, axis=-1, keepdims=True))
    return (shaped * lax.rsqrt(squares + EPSILON) * scale_row[:, None]).reshape(values.shape)

def key_table(keyval, head_count):
    width = keyval.shape[-1] // 2
    unit = jnp.ones((head_count,), jnp.float32)
    normed_keys = normalize_heads(keyval[..., :width].astype(jnp.float32), unit, head_count)
    return jnp.concatenate([normed_keys.astype(jnp.bfloat16), keyval[..., width:]], axis=-1)

def pool_level(keyval):
    height, breadth, channels = keyval.shape
    blocks = keyval.reshape(height // 2, 2, breadth // 2, 2, channels).astype(jnp.float32)
    return lax.optimization_barrier(jnp.mean(blocks, axis=(1, 3))).astype(jnp.bfloat16)

def attend(queries, keys_all, mask, head_count):
    tiles, q_count, width = queries.shape
    head_dim = width // head_count
    q_heads = queries.reshape(tiles, q_count, head_count, head_dim).astype(jnp.float32)
    k_heads = keys_all[..., :width].reshape(tiles, -1, head_count, head_dim).astype(jnp.float32)
    v_heads = keys_all[..., width:].reshape(tiles, -1, head_count, head_dim).astype(jnp.float32)
    scores = jnp.einsum('tqhd,tkhd->thqk', q_heads, k_heads)
    expo = jnp.exp(scores) * mask[:, None, None, :]
    weights = (expo / lax.optimization_barrier(jnp.sum(expo, axis=-1, keepdims=True))).astype(jnp.bfloat16)
    attended = jnp.einsum('thqk,tkhd->tqhd', weights.astype(jnp.float32), v_heads)
    return attended.astype(jnp.bfloat16).reshape(tiles, q_count, width)

def reference(tokens, ln_gain, w_query, w_keyval, logit_scale, w_output, parents, child_counts):
    total_rows, total_cols, width = tokens.shape
    head_count = logit_scale.shape[0]
    flat = tokens.reshape(-1, width).astype(jnp.float32)
    normed = layer_norm(flat, ln_gain).astype(jnp.bfloat16)
    query = jnp.dot(normed, w_query, preferred_element_type=jnp.float32)
    scaled = normalize_heads(query, logit_scale, head_count).astype(jnp.bfloat16)
    scaled = scaled.reshape(total_rows, total_cols, width)
    keyval = jnp.dot(normed, w_keyval, preferred_element_type=jnp.float32).astype(jnp.bfloat16)
    pyramid = [keyval.reshape(total_rows, total_cols, 2 * width)]
    for level_no in range(1, LEVELS):
        pyramid.append(pool_level(pyramid[-1]))
    tables = [key_table(layer, head_count) for layer in pyramid]
    tile_cols = total_cols // TILE

    def tile_split(strip):
        channels = strip.shape[-1]
        return strip.reshape(TILE, tile_cols, TILE, channels).transpose(1, 0, 2, 3).reshape(tile_cols, TILE * TILE, channels)

    def tile_row(row_no):
        queries = tile_split(lax.dynamic_slice_in_dim(scaled, row_no * TILE, TILE, 0))
        own_keys = tile_split(lax.dynamic_slice_in_dim(tables[0], row_no * TILE, TILE, 0))
        chosen_all = lax.dynamic_index_in_dim(parents, row_no, 0, keepdims=False)
        counts_all = lax.dynamic_index_in_dim(child_counts, row_no, 0, keepdims=False)
        key_parts = [own_keys]
        mask_parts = [jnp.ones((tile_cols, TILE * TILE), jnp.float32)]
        for level_no in range(LEVELS):
            cell_rows = ROWS_DEV >> level_no + 1
            cell_cols = COLS_DEV >> level_no + 1
            chosen = chosen_all[:, level_no, :]
            home_dev = chosen // (cell_rows * cell_cols)
            local_cell = chosen % (cell_rows * cell_cols)
            par_row = home_dev // N_COL * cell_rows + local_cell // cell_cols
            par_col = home_dev % N_COL * cell_cols + local_cell % cell_cols
            child_rows = jnp.stack([2 * par_row + offset for offset in (0, 0, 1, 1)], axis=-1)
            child_cols = jnp.stack([2 * par_col + offset for offset in (0, 1, 0, 1)], axis=-1)
            gathered = tables[level_no][child_rows, child_cols]
            key_parts.append(gathered.reshape(tile_cols, TOPK * 4, 2 * width))
            ranks = jnp.arange(4, dtype=jnp.int32)
            valid = (ranks[None, None, :] < counts_all[:, level_no, :, None]).astype(jnp.float32)
            mask_parts.append(valid.reshape(tile_cols, TOPK * 4))
        keys_all = jnp.concatenate(key_parts, axis=1)
        mask = jnp.concatenate(mask_parts, axis=1)
        attended = attend(queries, keys_all, mask, head_count)
        return attended.reshape(tile_cols, TILE, TILE, width).transpose(1, 0, 2, 3).reshape(TILE, total_cols, width)
    rows_out = lax.map(tile_row, jnp.arange(total_rows // TILE, dtype=jnp.int32))
    attended = rows_out.reshape(-1, width)
    mixed = jnp.dot(attended, w_output, preferred_element_type=jnp.float32).astype(jnp.bfloat16)
    return mixed.reshape(total_rows, total_cols, width)
```

```python
import functools

import jax
import jax.numpy as jnp
from jax import lax
from jax.experimental import pallas as pl
from jax.experimental.pallas import tpu as pltpu
from jax.sharding import PartitionSpec as P

TILE = 8
LEVELS = 3
TOPK = 8
EPSILON = 1e-06
F32 = jnp.float32
BF16 = jnp.bfloat16
MESH = pl.DeviceIdType.MESH

DEVICES = 128
N_COL = 16
SIDE = 32
TOKENS = SIDE * SIDE
TILES = 16
REQUESTS = TILES * TOPK
WIDTH = 1024
HALF = WIDTH // 2
HEAD = 64
GROUP = 256
OWN = TILE * TILE
PER_LEVEL = TOPK * 4
KEYS = OWN + LEVELS * PER_LEVEL
STEP = 37
SERVED = 32


def shifted(place, sign):
    offset = lax.rem(place * STEP, DEVICES)
    row, col = lax.axis_index("row"), lax.axis_index("col")
    core = lax.rem(lax.rem(row, 2) + lax.rem(offset, 2), 2)
    x = lax.rem(lax.rem(col, 4) + sign * lax.rem(offset // 2, 4) + 4, 4)
    z = lax.rem(col // 4 + sign * lax.rem(offset // 8, 4) + 4, 4)
    y = lax.rem(row // 2 + sign * (offset // 32) + 4, 4)
    return y * 2 + core, z * 4 + x


def iota(shape, axis):
    return lax.broadcasted_iota(jnp.int32, shape, axis)


def ones_where(condition):
    return jnp.where(condition, 1.0, 0.0)


def dot(a, b):
    return jnp.dot(a, b, preferred_element_type=F32)


def same_head():
    return ones_where(iota((GROUP, GROUP), 0) // HEAD == iota((GROUP, GROUP), 1) // HEAD).astype(BF16)


def unit_heads(values, block_ones):
    squares = values * values
    high = squares.astype(BF16)
    low = (squares - high.astype(F32)).astype(BF16)
    total = dot(high, block_ones) + dot(low, block_ones)
    return values * lax.rsqrt(total + EPSILON)


def column_of(raw_ref, level):
    raw = raw_ref[...].reshape(TILES, LEVELS, TOPK)[:, level : level + 1, :].astype(F32)
    spread = jnp.broadcast_to(raw, (TILES, TOPK, TOPK))
    keep = iota((TILES, TOPK, TOPK), 1) == iota((TILES, TOPK, TOPK), 2)
    return jnp.sum(jnp.where(keep, spread, 0.0), axis=2, keepdims=True).reshape(REQUESTS, 1)


def row_of(column):
    square = (REQUESTS, REQUESTS)
    spread = jnp.broadcast_to(column, square)
    return jnp.sum(jnp.where(iota(square, 0) == iota(square, 1), spread, 0.0), axis=0, keepdims=True)


def kernel(
    tokens_hbm, gain_ref, w_query_hbm, w_keyval_hbm, scale_ref, w_output_hbm, parents_ref, counts_ref,
    out_ref,
    tokens, w_query, w_keyval, w_output, normed, queries, keys, values, marks, attended, picked,
    ask, asked, send, recv, place_of,
    load_sem, ask_send, ask_recv, reply_send, reply_recv, self_sem,
):
    square = (REQUESTS, REQUESTS)
    loads = [
        pltpu.make_async_copy(source, target, load_sem.at[number])
        for number, (source, target) in enumerate(
            ((tokens_hbm, tokens), (w_keyval_hbm, w_keyval), (w_query_hbm, w_query), (w_output_hbm, w_output))
        )
    ]
    for load in loads:
        load.start()

    barrier = pltpu.get_barrier_semaphore()

    def greet(place, carry):
        pl.semaphore_signal(barrier, inc=1, device_id=shifted(place, 1), device_id_type=MESH)
        return carry

    lax.fori_loop(1, DEVICES, greet, 0)

    lane = iota(square, 1)
    lane_level, lane_slot, lane_child = lane // 8, lane // 4 % 2, lane % 4
    table = jnp.zeros(square, F32)
    for level in range(LEVELS):
        parent_col = column_of(parents_ref, level).astype(jnp.int32)
        parent_row = row_of(parent_col.astype(F32)).astype(jnp.int32)
        bits = 8 - 2 * level
        home_col, home_row = parent_col >> bits, parent_row >> bits
        local_row = (parent_row & ((1 << bits) - 1)).astype(F32)
        same = home_col == home_row
        rank_col = jnp.sum(ones_where(same & (iota(square, 1) < iota(square, 0))), axis=1, keepdims=True)
        rank_row = jnp.sum(ones_where(same & (iota(square, 0) < iota(square, 1))), axis=0, keepdims=True)
        place_of[level] = jnp.broadcast_to(home_col * 8 + rank_col.astype(jnp.int32) * 4, square)
        for slot in range(2):
            here = (iota(square, 0) == home_row) & (rank_row == float(slot))
            cell = jnp.sum(jnp.where(here, local_row, 0.0), axis=1, keepdims=True)
            table = jnp.where((lane_level == level) & (lane_slot == slot), cell, table)
    local = table.astype(jnp.int32)
    wide_bits = 4 - lane_level
    parent_r, parent_c = local >> wide_bits, local & ((1 << wide_bits) - 1)
    child = ((2 * parent_r + lane_child // 2) << (wide_bits + 1)) + 2 * parent_c + lane_child % 2
    ask[...] = child.reshape(DEVICES, 1, REQUESTS)

    me = lax.axis_index("row") * N_COL + lax.axis_index("col")
    own_ask = pltpu.make_async_copy(ask.at[me], asked.at[0], self_sem.at[LEVELS])
    own_ask.start()
    pl.semaphore_wait(barrier, DEVICES - 1)

    def send_ask(place, carry):
        row, col = shifted(place, -1)
        pltpu.make_async_remote_copy(
            src_ref=ask.at[row * N_COL + col], dst_ref=asked.at[place], send_sem=ask_send, recv_sem=ask_recv,
            device_id=(row, col), device_id_type=MESH,
        ).start()
        return carry

    lax.fori_loop(1, DEVICES, send_ask, 0)

    loads[0].wait()
    gain = gain_ref[...].reshape(1, WIDTH)

    def norm_rows(pair, carry):
        flat = tokens[pl.ds(2 * pair, 2)].reshape(2 * SIDE, WIDTH).astype(F32)
        centered = flat - jnp.mean(flat, axis=1, keepdims=True)
        spread = jnp.mean(centered * centered, axis=1, keepdims=True)
        result = centered * lax.rsqrt(spread + EPSILON) * gain
        tiled = result.reshape(2, 4, TILE, WIDTH).transpose(1, 0, 2, 3).reshape(4, 16, WIDTH).astype(BF16)
        for tile in range(4):
            start = pl.multiple_of((pair // 4 * 4 + tile) * OWN + pair % 4 * 16, 16)
            normed[pl.ds(start, 16), :] = tiled[tile]
        return carry

    lax.fori_loop(0, SIDE // 2, norm_rows, 0)

    own_ask.wait()
    pltpu.make_async_remote_copy(
        src_ref=ask.at[pl.ds(0, DEVICES - 1)], dst_ref=asked.at[pl.ds(0, DEVICES - 1)], send_sem=ask_send,
        recv_sem=ask_recv, device_id=shifted(1, 1), device_id_type=MESH,
    ).wait()
    token = iota((1, TOKENS), 1)
    token_r = token // 256 * 8 + token // 8 % 8
    token_c = token // 64 % 4 * 8 + token % 8
    place_in_eight = iota((SERVED, 8, REQUESTS), 1)
    lane_in_eight = iota((SERVED, 8, REQUESTS), 2)
    for level in range(LEVELS):
        cell_of = (token_r >> level) * (SIDE >> level) + (token_c >> level)

        def serve(block, carry):
            first = pl.multiple_of(block * SERVED, SERVED)
            wanted = jnp.broadcast_to(asked[pl.ds(first, SERVED)].astype(F32), (SERVED, 8, REQUESTS))
            wanted = jnp.where(lane_in_eight == place_in_eight + 8 * level, wanted, 0.0)
            wanted = jnp.sum(wanted, axis=2, keepdims=True).reshape(SERVED * 8, 1).astype(jnp.int32)
            pick = jnp.where(wanted == cell_of, 0.25**level, 0.0).astype(BF16)
            left = dot(pick, normed[:, :HALF]).reshape(SERVED, 8, HALF)
            right = dot(pick, normed[:, HALF:]).reshape(SERVED, 8, HALF)
            send[level, pl.ds(first, SERVED)] = jnp.concatenate([left, right], axis=1).astype(BF16)

            def send_reply(place, carry):
                row, col = shifted(place, 1)
                pltpu.make_async_remote_copy(
                    src_ref=send.at[level, place], dst_ref=recv.at[level, me], send_sem=reply_send.at[level],
                    recv_sem=reply_recv.at[level], device_id=(row, col), device_id_type=MESH,
                ).start()
                return carry

            lax.fori_loop(jnp.maximum(first, 1), first + SERVED, send_reply, 0)
            return carry

        lax.fori_loop(0, DEVICES // SERVED, serve, 0)
        pltpu.make_async_copy(send.at[level, 0], recv.at[level, me], self_sem.at[level]).start()

    block_ones = same_head()
    loads[1].wait()
    loads[2].wait()

    def project(block, carry):
        rows = pl.ds(pl.multiple_of(block * GROUP, GROUP), GROUP)
        tiles = pl.ds(block * 4, 4)
        flat = normed[rows, :]
        for group in range(WIDTH // GROUP):
            span = slice(group * GROUP, (group + 1) * GROUP)
            query = unit_heads(dot(flat, w_query[:, span]), block_ones) * scale_ref[:, span]
            queries[rows, span] = query.astype(BF16)
            key = dot(flat, w_keyval[:, span]).astype(BF16).astype(F32)
            keys[tiles, 0:OWN, span] = unit_heads(key, block_ones).astype(BF16).reshape(4, OWN, GROUP)
            value = dot(flat, w_keyval[:, WIDTH + group * GROUP : WIDTH + (group + 1) * GROUP])
            values[tiles, 0:OWN, span] = value.astype(BF16).reshape(4, OWN, GROUP)
        return carry

    lax.fori_loop(0, TOKENS // GROUP, project, 0)
    marks[:, 0:OWN, :] = jnp.ones((TILES, OWN, REQUESTS), BF16)

    def by_tile(rows):
        columns = rows.shape[-1]
        return rows.reshape(4, TILES, TOPK, columns).transpose(1, 0, 2, 3).reshape(TILES, PER_LEVEL, columns)

    slots = iota((REQUESTS, DEVICES * 8), 1)
    for level in range(LEVELS):
        pltpu.make_async_copy(send.at[level, 0], recv.at[level, me], self_sem.at[level]).wait()
        pltpu.make_async_remote_copy(
            src_ref=send.at[level, pl.ds(0, DEVICES - 1)], dst_ref=recv.at[level, pl.ds(0, DEVICES - 1)],
            send_sem=reply_send.at[level], recv_sem=reply_recv.at[level], device_id=shifted(1, 1),
            device_id_type=MESH,
        ).wait()
        count_col = column_of(counts_ref, level)
        place_col = place_of[level][:, 0:1]
        valid = [count_col > float(child) for child in range(4)]
        marks[:, OWN + level * PER_LEVEL : OWN + (level + 1) * PER_LEVEL, :] = by_tile(
            jnp.concatenate([jnp.broadcast_to(ones_where(flag), square) for flag in valid], axis=0)
        ).astype(BF16)
        for side in range(2):
            rows = recv[level].astype(F32)[:, side * 8 : side * 8 + 8, :].reshape(DEVICES * 8, HALF).astype(BF16)
            for child in range(4):
                pick = ones_where((slots == place_col + child) & valid[child]).astype(BF16)
                picked[child * REQUESTS : (child + 1) * REQUESTS, side * HALF : (side + 1) * HALF] = dot(
                    pick, rows
                ).astype(BF16)
        span_rows = slice(OWN + level * PER_LEVEL, OWN + (level + 1) * PER_LEVEL)
        for group in range(WIDTH // GROUP):
            span = slice(group * GROUP, (group + 1) * GROUP)
            key = dot(picked[...], w_keyval[:, span]).astype(BF16).astype(F32)
            keys[:, span_rows, span] = by_tile(unit_heads(key, block_ones)).astype(BF16)
            value = dot(picked[...], w_keyval[:, WIDTH + group * GROUP : WIDTH + (group + 1) * GROUP])
            values[:, span_rows, span] = by_tile(value).astype(BF16)

    loads[3].wait()
    head_of = iota((OWN, GROUP), 1) // HEAD

    def four_tiles(block, carry):
        def one_tile(tile, carry):
            rows = pl.ds(pl.multiple_of(tile * OWN, OWN), OWN)
            for group in range(WIDTH // GROUP):
                span = slice(group * GROUP, (group + 1) * GROUP)
                query = queries[rows, span].astype(F32)
                stacked = jnp.concatenate(
                    [jnp.where(head_of == head, query, 0.0).astype(BF16) for head in range(4)], axis=0
                )
                score = lax.dot_general(
                    stacked, keys[tile, :, span], (((1,), (1,)), ((), ())), preferred_element_type=F32
                )
                weight = jnp.exp(score).astype(BF16)
                total = dot(weight, marks[tile])
                total = jnp.concatenate([total, total], axis=1)
                mixed = dot(weight, values[tile, :, span])
                top, bottom = mixed[0:OWN], total[0:OWN]
                for head in range(1, 4):
                    top = jnp.where(head_of == head, mixed[head * OWN : (head + 1) * OWN], top)
                    bottom = jnp.where(head_of == head, total[head * OWN : (head + 1) * OWN], bottom)
                attended[rows, span] = (top / bottom).astype(BF16)
            return carry

        lax.fori_loop(block * 4, block * 4 + 4, one_tile, 0)
        flat = attended[pl.ds(pl.multiple_of(block * GROUP, GROUP), GROUP), :]
        for side in range(2):
            span = slice(side * HALF, (side + 1) * HALF)
            mixed = dot(flat, w_output[:, span]).reshape(4, TILE, TILE, HALF)
            mixed = mixed.transpose(1, 0, 2, 3).reshape(TILE, SIDE, HALF).astype(BF16)
            out_ref[pl.ds(block * TILE, TILE), :, span] = mixed
        return carry

    lax.fori_loop(0, TILES // 4, four_tiles, 0)


def per_device(tokens, ln_gain, w_query, w_keyval, logit_scale, w_output, parents, child_counts):
    scale_row = jnp.repeat(logit_scale, HEAD).reshape(1, WIDTH)
    whole = pl.BlockSpec(memory_space=pltpu.VMEM)
    anywhere = pl.BlockSpec(memory_space=pl.ANY)
    return pl.pallas_call(
        kernel,
        out_shape=jax.ShapeDtypeStruct((SIDE, SIDE, WIDTH), BF16),
        in_specs=[anywhere, whole, anywhere, anywhere, whole, anywhere, whole, whole],
        out_specs=whole,
        scratch_shapes=[
            pltpu.VMEM((SIDE, SIDE, WIDTH), BF16),
            pltpu.VMEM((WIDTH, WIDTH), BF16),
            pltpu.VMEM((WIDTH, 2 * WIDTH), BF16),
            pltpu.VMEM((WIDTH, WIDTH), BF16),
            pltpu.VMEM((TOKENS, WIDTH), BF16),
            pltpu.VMEM((TOKENS, WIDTH), BF16),
            pltpu.VMEM((TILES, KEYS, WIDTH), BF16),
            pltpu.VMEM((TILES, KEYS, WIDTH), BF16),
            pltpu.VMEM((TILES, KEYS, REQUESTS), BF16),
            pltpu.VMEM((TOKENS, WIDTH), BF16),
            pltpu.VMEM((4 * REQUESTS, WIDTH), BF16),
            pltpu.VMEM((DEVICES, 1, REQUESTS), jnp.int32),
            pltpu.VMEM((DEVICES, 1, REQUESTS), jnp.int32),
            pltpu.VMEM((LEVELS, DEVICES, 16, HALF), BF16),
            pltpu.VMEM((LEVELS, DEVICES, 16, HALF), BF16),
            pltpu.VMEM((LEVELS, REQUESTS, REQUESTS), jnp.int32),
            pltpu.SemaphoreType.DMA((4,)),
            pltpu.SemaphoreType.DMA,
            pltpu.SemaphoreType.DMA,
            pltpu.SemaphoreType.DMA((LEVELS,)),
            pltpu.SemaphoreType.DMA((LEVELS,)),
            pltpu.SemaphoreType.DMA((LEVELS + 1,)),
        ],
        compiler_params=pltpu.CompilerParams(
            collective_id=0, has_side_effects=True, vmem_limit_bytes=60 * 2**20
        ),
    )(tokens, ln_gain, w_query, w_keyval, scale_row, w_output, parents, child_counts)


def solution(mesh):
    in_specs = (
        P("row", "col", None),
        P(),
        P(),
        P(),
        P(),
        P(),
        P("row", "col", None, None),
        P("row", "col", None, None),
    )
    return jax.shard_map(
        per_device, mesh=mesh, in_specs=in_specs, out_specs=P("row", "col", None), check_vma=False
    )
```

```python
import functools

import jax
import jax.numpy as jnp
from jax import lax
from jax.experimental import pallas as pl
from jax.experimental.pallas import tpu as pltpu
from jax.sharding import PartitionSpec as P

TILE = 8
LEVELS = 3
TOPK = 8
EPSILON = 1e-06
F32 = jnp.float32
BF16 = jnp.bfloat16
MESH = pl.DeviceIdType.MESH

DEVICES = 128
N_COL = 16
SIDE = 32
TOKENS = SIDE * SIDE
TILES = 16
REQUESTS = TILES * TOPK
WIDTH = 1024
HALF = WIDTH // 2
HEAD = 64
GROUP = 256
OWN = TILE * TILE
PER_LEVEL = TOPK * 4
KEYS = OWN + LEVELS * PER_LEVEL
N_ROW = 8
SERVED = 32


def wrap(value):
    return jnp.where(value >= 4, value - 4, value)


def row_shifted(place):
    row = lax.axis_index("row")
    y, core = lax.div(row, 2), lax.rem(row, 2)
    return wrap(y + place // 2) * 2 + (1 - core if place % 2 else core)


def col_shifted(place, sign):
    col = lax.axis_index("col")
    off_z = place % 4
    off_x = (place // 4 + 3 * off_z) % 4
    z = wrap(lax.div(col, 4) + (sign * off_z) % 4)
    x = wrap(lax.rem(col, 4) + (sign * off_x) % 4)
    return z * 4 + x


def iota(shape, axis):
    return lax.broadcasted_iota(jnp.int32, shape, axis)


def ones_where(condition):
    return jnp.where(condition, 1.0, 0.0)


def dot(a, b):
    return jnp.dot(a, b, preferred_element_type=F32)


def dot_rows(a, b):
    return lax.dot_general(a, b, (((1,), (1,)), ((), ())), preferred_element_type=F32)


def same_head():
    return ones_where(iota((GROUP, GROUP), 0) // HEAD == iota((GROUP, GROUP), 1) // HEAD).astype(BF16)


def unit_heads(values, block_ones):
    squares = values * values
    high = squares.astype(BF16)
    low = (squares - high.astype(F32)).astype(BF16)
    total = dot(high, block_ones) + dot(low, block_ones)
    return values * lax.rsqrt(total + EPSILON)


def column_of(raw_ref, level):
    raw = raw_ref[:, level].astype(F32).reshape(TILES, 1, TOPK)
    spread = jnp.broadcast_to(raw, (TILES, TOPK, TOPK))
    keep = iota((TILES, TOPK, TOPK), 1) == iota((TILES, TOPK, TOPK), 2)
    return jnp.sum(jnp.where(keep, spread, 0.0), axis=2, keepdims=True).reshape(REQUESTS, 1)


def row_of(column):
    square = (REQUESTS, REQUESTS)
    spread = jnp.broadcast_to(column, square)
    return jnp.sum(jnp.where(iota(square, 0) == iota(square, 1), spread, 0.0), axis=0, keepdims=True)


def kernel(
    tokens_hbm, gain_ref, w_query_hbm, w_keyval_hbm, scale_ref, parents_ref, counts_ref,
    attended,
    tokens, w_query, w_keyval, normed, queries, keys, values, marks, summed, weighed, picked,
    ask, passed, asked, send, recv, place_of,
    load_sem, pass_send, pass_recv, ask_send, ask_recv, reply_send, reply_recv, self_sem,
):
    square = (REQUESTS, REQUESTS)
    loads = [
        pltpu.make_async_copy(source, target, load_sem.at[number])
        for number, (source, target) in enumerate(
            ((tokens_hbm, tokens), (w_keyval_hbm, w_keyval), (w_query_hbm, w_query))
        )
    ]
    for load in loads:
        load.start()

    barrier = pltpu.get_barrier_semaphore()

    row, col = lax.axis_index("row"), lax.axis_index("col")
    me = row * N_COL + col

    rows_at = [row_shifted(place) for place in range(N_ROW)]
    cols_at = [col_shifted(place, 1) for place in range(N_COL)]
    for place in range(1, N_ROW):
        pl.semaphore_signal(barrier, inc=1, device_id=(rows_at[place], col), device_id_type=MESH)
    for place in range(1, N_COL):
        pl.semaphore_signal(barrier, inc=1, device_id=(row, cols_at[place]), device_id_type=MESH)

    lane = iota(square, 1)
    lane_level, lane_slot, lane_child = lane // 8, lane // 4 % 2, lane % 4
    table = jnp.zeros(square, F32)
    for level in range(LEVELS):
        parent_col = column_of(parents_ref, level).astype(jnp.int32)
        parent_row = row_of(parent_col.astype(F32)).astype(jnp.int32)
        bits = 8 - 2 * level
        home_col, home_row = parent_col >> bits, parent_row >> bits
        local_row = (parent_row & ((1 << bits) - 1)).astype(F32)
        same = home_col == home_row
        rank_col = jnp.sum(ones_where(same & (iota(square, 1) < iota(square, 0))), axis=1, keepdims=True)
        rank_row = jnp.sum(ones_where(same & (iota(square, 0) < iota(square, 1))), axis=0, keepdims=True)
        place_of[level] = jnp.broadcast_to(home_col * 8 + rank_col.astype(jnp.int32) * 4, square)
        for slot in range(2):
            here = (iota(square, 0) == home_row) & (rank_row == float(slot))
            cell = jnp.sum(jnp.where(here, local_row, 0.0), axis=1, keepdims=True)
            table = jnp.where((lane_level == level) & (lane_slot == slot), cell, table)
    local = table.astype(jnp.int32)
    wide_bits = 4 - lane_level
    parent_r, parent_c = local >> wide_bits, local & ((1 << wide_bits) - 1)
    child = ((2 * parent_r + lane_child // 2) << (wide_bits + 1)) + 2 * parent_c + lane_child % 2
    ask[...] = child.reshape(DEVICES, 1, REQUESTS)

    own_pass = pltpu.make_async_copy(ask.at[pl.ds(row * N_COL, N_COL)], passed.at[row], self_sem.at[LEVELS])
    own_pass.start()
    pl.semaphore_wait(barrier, N_ROW + N_COL - 2)

    for place in range(1, N_ROW):
        pltpu.make_async_remote_copy(
            src_ref=ask.at[pl.ds(rows_at[place] * N_COL, N_COL)], dst_ref=passed.at[row], send_sem=pass_send,
            recv_sem=pass_recv, device_id=(rows_at[place], col), device_id_type=MESH,
        ).start()

    loads[0].wait()
    gain = gain_ref[...].reshape(1, WIDTH)

    def norm_rows(pair, carry):
        flat = tokens[pl.ds(2 * pair, 2)].reshape(2 * SIDE, WIDTH).astype(F32)
        centered = flat - jnp.mean(flat, axis=1, keepdims=True)
        spread = jnp.mean(centered * centered, axis=1, keepdims=True)
        result = centered * lax.rsqrt(spread + EPSILON) * gain
        tiled = result.reshape(2, 4, TILE, WIDTH).transpose(1, 0, 2, 3).reshape(4, 16, WIDTH).astype(BF16)
        for tile in range(4):
            start = pl.multiple_of((pair // 4 * 4 + tile) * OWN + pair % 4 * 16, 16)
            normed[pl.ds(start, 16), :] = tiled[tile]
        return carry

    lax.fori_loop(0, SIDE // 4, norm_rows, 0)
    own_pass.wait()
    pltpu.make_async_remote_copy(
        src_ref=passed.at[pl.ds(0, N_ROW - 1)], dst_ref=passed.at[pl.ds(0, N_ROW - 1)], send_sem=pass_send,
        recv_sem=pass_recv, device_id=(rows_at[1], col), device_id_type=MESH,
    ).wait()
    own_ask = pltpu.make_async_copy(passed.at[:, col], asked.at[0], self_sem.at[LEVELS])
    own_ask.start()

    for place in range(1, N_COL):
        to = col_shifted(place, -1)
        pltpu.make_async_remote_copy(
            src_ref=passed.at[:, to], dst_ref=asked.at[place], send_sem=ask_send, recv_sem=ask_recv,
            device_id=(row, to), device_id_type=MESH,
        ).start()

    lax.fori_loop(SIDE // 4, SIDE // 2, norm_rows, 0)

    own_ask.wait()
    pltpu.make_async_remote_copy(
        src_ref=asked.at[pl.ds(0, N_COL - 1)], dst_ref=asked.at[pl.ds(0, N_COL - 1)], send_sem=ask_send,
        recv_sem=ask_recv, device_id=(row, cols_at[1]), device_id_type=MESH,
    ).wait()
    token = iota((1, TOKENS), 1)
    token_r = token // 256 * 8 + token // 8 % 8
    token_c = token // 64 % 4 * 8 + token % 8
    place_in_eight = iota((SERVED, 8, REQUESTS), 1)
    lane_in_eight = iota((SERVED, 8, REQUESTS), 2)

    def gather(levels, block):
        first = pl.multiple_of(block * SERVED, SERVED)
        asks = asked[pl.ds(block * 4, 4)].astype(F32).reshape(SERVED, 1, REQUESTS)
        asks = jnp.broadcast_to(asks, (SERVED, 8, REQUESTS))
        picks = []
        for level in levels:
            cell_of = (token_r >> level) * (SIDE >> level) + (token_c >> level)
            wanted = jnp.where(lane_in_eight == place_in_eight + 8 * level, asks, 0.0)
            wanted = jnp.sum(wanted, axis=2, keepdims=True).reshape(SERVED * 8, 1).astype(jnp.int32)
            picks.append(jnp.where(wanted == cell_of, 0.25**level, 0.0).astype(BF16))
        pick = jnp.concatenate(picks, axis=0)
        left = dot(pick, normed[:, :HALF]).reshape(len(levels), SERVED, 8, HALF)
        right = dot(pick, normed[:, HALF:]).reshape(len(levels), SERVED, 8, HALF)
        for number, level in enumerate(levels):
            both = jnp.concatenate([left[number], right[number]], axis=1)
            send[level, pl.ds(first, SERVED)] = both.astype(BF16)

    def send_replies(level, blocks):
        for turn in range(SERVED * len(blocks)):
            block, off_z = blocks[turn // SERVED], turn % 4
            place = (turn // 4 + off_z) % 4 * 2 + turn % SERVED // 16
            if block == 0 and off_z == 0 and place == 0:
                continue
            pltpu.make_async_remote_copy(
                src_ref=send.at[level, block * SERVED + off_z * N_ROW + rows_at[place]],
                dst_ref=recv.at[level, me], send_sem=reply_send.at[level], recv_sem=reply_recv.at[level],
                device_id=(rows_at[place], cols_at[block * 4 + off_z]), device_id_type=MESH,
            ).start()

    def own_reply(level):
        return pltpu.make_async_copy(send.at[level, row], recv.at[level, me], self_sem.at[level])

    def gather_later(block, carry):
        gather((1, 2), block)
        return carry

    for block in range(DEVICES // SERVED):
        gather((0,), block)
        send_replies(0, (block,))
    lax.fori_loop(0, DEVICES // SERVED, gather_later, 0)
    send_replies(1, range(DEVICES // SERVED))
    for level in range(LEVELS):
        own_reply(level).start()

    block_ones = same_head()
    loads[1].wait()
    loads[2].wait()

    def project(block, carry):
        rows = pl.ds(pl.multiple_of(block * HALF, HALF), HALF)
        tiles = pl.ds(block * 8, 8)
        flat = normed[rows, :]
        for group in range(WIDTH // GROUP):
            span = slice(group * GROUP, (group + 1) * GROUP)
            scale = jnp.zeros((1, GROUP), F32)
            for head in range(4):
                scale = jnp.where(iota((1, GROUP), 1) // HEAD == head, scale_ref[group * 4 + head], scale)
            query = unit_heads(dot(flat, w_query[:, span]), block_ones) * scale
            queries[rows, span] = query.astype(BF16)
            key = dot(flat, w_keyval[:, span]).astype(BF16).astype(F32)
            keys[tiles, 0:OWN, span] = unit_heads(key, block_ones).astype(BF16).reshape(8, OWN, GROUP)
            value = dot(flat, w_keyval[:, WIDTH + group * GROUP : WIDTH + (group + 1) * GROUP])
            values[tiles, 0:OWN, span] = value.astype(BF16).reshape(8, OWN, GROUP)
        return carry

    lax.fori_loop(0, TOKENS // HALF, project, 0)
    marks[:, 0:OWN, :] = jnp.ones((TILES, OWN, REQUESTS), BF16)
    send_replies(2, range(DEVICES // SERVED))

    def by_tile(rows):
        columns = rows.shape[-1]
        return rows.reshape(4, TILES, TOPK, columns).transpose(1, 0, 2, 3).reshape(TILES, PER_LEVEL, columns)

    slots = iota((REQUESTS, DEVICES * 8), 1)
    early = OWN + (LEVELS - 1) * PER_LEVEL

    def sums_over(tile, group, first, last):
        masks = [ones_where(iota((last - first, GROUP), 1) // HEAD == head).astype(BF16) for head in range(4)]
        rows = pl.ds(pl.multiple_of(tile * OWN, OWN), OWN)
        span = slice(group * GROUP, (group + 1) * GROUP)
        key, value, mark = keys[tile, first:last, span], values[tile, first:last, span], marks[tile, first:last]
        mark = jnp.concatenate([mark, mark], axis=1)
        key, value, mark = [jnp.concatenate([part * mask for mask in masks], axis=0) for part in (key, value, mark)]
        weight = jnp.exp(dot_rows(queries[rows, span], key)).astype(BF16)
        return rows, span, dot(weight, value), dot(weight, mark)

    def own_keys(tile, carry):
        for group in range(WIDTH // GROUP):
            rows, span, top, bottom = sums_over(tile, group, 0, OWN)
            summed[rows, span] = top
            weighed[rows, span] = bottom
        return carry

    def early_keys(tile, carry):
        for group in range(WIDTH // GROUP):
            rows, span, top, bottom = sums_over(tile, group, OWN, early)
            summed[rows, span] += top
            weighed[rows, span] += bottom
        return carry

    lax.fori_loop(0, TILES, own_keys, 0, unroll=2)
    for level in range(LEVELS):
        if level == 2:
            lax.fori_loop(0, TILES, early_keys, 0, unroll=2)
        own_reply(level).wait()
        pltpu.make_async_remote_copy(
            src_ref=send.at[level, pl.ds(0, DEVICES - 1)], dst_ref=recv.at[level, pl.ds(0, DEVICES - 1)],
            send_sem=reply_send.at[level], recv_sem=reply_recv.at[level],
            device_id=(rows_at[1], col), device_id_type=MESH,
        ).wait()
        count_col = column_of(counts_ref, level)
        place_col = place_of[level][:, 0:1]
        valid = [count_col > float(child) for child in range(4)]
        marks[:, OWN + level * PER_LEVEL : OWN + (level + 1) * PER_LEVEL, :] = by_tile(
            jnp.concatenate([jnp.broadcast_to(ones_where(flag), square) for flag in valid], axis=0)
        ).astype(BF16)
        pick = jnp.concatenate(
            [ones_where((slots == place_col + child) & valid[child]).astype(BF16) for child in range(4)], axis=0
        )
        for side in range(2):
            rows = recv[level].astype(F32)[:, side * 8 : side * 8 + 8, :].reshape(DEVICES * 8, HALF).astype(BF16)
            picked[:, side * HALF : (side + 1) * HALF] = dot(pick, rows).astype(BF16)
        span_rows = slice(OWN + level * PER_LEVEL, OWN + (level + 1) * PER_LEVEL)
        for group in range(WIDTH // GROUP):
            span = slice(group * GROUP, (group + 1) * GROUP)
            key = dot(picked[...], w_keyval[:, span]).astype(BF16).astype(F32)
            keys[:, span_rows, span] = by_tile(unit_heads(key, block_ones)).astype(BF16)
            value = dot(picked[...], w_keyval[:, WIDTH + group * GROUP : WIDTH + (group + 1) * GROUP])
            values[:, span_rows, span] = by_tile(value).astype(BF16)

    def last_keys(tile, carry):
        for group in range(WIDTH // GROUP):
            rows, span, top, bottom = sums_over(tile, group, early, KEYS)
            attended[rows, span] = ((summed[rows, span] + top) / (weighed[rows, span] + bottom)).astype(BF16)
        return carry

    lax.fori_loop(0, TILES, last_keys, 0, unroll=2)


def mix(attended, w_output, out_ref):
    mixed = dot(attended[...], w_output[...]).reshape(4, TILE, TILE, WIDTH)
    out_ref[...] = mixed.transpose(1, 0, 2, 3).reshape(TILE, SIDE, WIDTH).astype(BF16)


def per_device(tokens, ln_gain, w_query, w_keyval, logit_scale, w_output, parents, child_counts):
    whole = pl.BlockSpec(memory_space=pltpu.VMEM)
    anywhere = pl.BlockSpec(memory_space=pl.ANY)
    attended = pl.pallas_call(
        kernel,
        out_shape=jax.ShapeDtypeStruct((TOKENS, WIDTH), BF16),
        in_specs=[anywhere, whole, anywhere, anywhere, pl.BlockSpec(memory_space=pltpu.SMEM), whole, whole],
        out_specs=whole,
        scratch_shapes=[
            pltpu.VMEM((SIDE, SIDE, WIDTH), BF16),
            pltpu.VMEM((WIDTH, WIDTH), BF16),
            pltpu.VMEM((WIDTH, 2 * WIDTH), BF16),
            pltpu.VMEM((TOKENS, WIDTH), BF16),
            pltpu.VMEM((TOKENS, WIDTH), BF16),
            pltpu.VMEM((TILES, KEYS, WIDTH), BF16),
            pltpu.VMEM((TILES, KEYS, WIDTH), BF16),
            pltpu.VMEM((TILES, KEYS, REQUESTS), BF16),
            pltpu.VMEM((TOKENS, WIDTH), F32),
            pltpu.VMEM((TOKENS, WIDTH), F32),
            pltpu.VMEM((4 * REQUESTS, WIDTH), BF16),
            pltpu.VMEM((DEVICES, 1, REQUESTS), jnp.int32),
            pltpu.VMEM((N_ROW, N_COL, 1, REQUESTS), jnp.int32),
            pltpu.VMEM((N_COL, N_ROW, 1, REQUESTS), jnp.int32),
            pltpu.VMEM((LEVELS, DEVICES, 16, HALF), BF16),
            pltpu.VMEM((LEVELS, DEVICES, 16, HALF), BF16),
            pltpu.VMEM((LEVELS, REQUESTS, REQUESTS), jnp.int32),
            pltpu.SemaphoreType.DMA((3,)),
            pltpu.SemaphoreType.DMA,
            pltpu.SemaphoreType.DMA,
            pltpu.SemaphoreType.DMA,
            pltpu.SemaphoreType.DMA,
            pltpu.SemaphoreType.DMA((LEVELS,)),
            pltpu.SemaphoreType.DMA((LEVELS,)),
            pltpu.SemaphoreType.DMA((LEVELS + 1,)),
        ],
        compiler_params=pltpu.CompilerParams(
            collective_id=0, has_side_effects=True, vmem_limit_bytes=60 * 2**20
        ),
    )(tokens, ln_gain, w_query, w_keyval, logit_scale, parents.transpose(0, 2, 1, 3), child_counts.transpose(0, 2, 1, 3))
    return pl.pallas_call(
        mix,
        grid=(TILES // 4,),
        out_shape=jax.ShapeDtypeStruct((SIDE, SIDE, WIDTH), BF16),
        in_specs=[
            pl.BlockSpec((4 * OWN, WIDTH), lambda block: (block, 0)),
            pl.BlockSpec((WIDTH, WIDTH), lambda block: (0, 0)),
        ],
        out_specs=pl.BlockSpec((TILE, SIDE, WIDTH), lambda block: (block, 0, 0)),
        compiler_params=pltpu.CompilerParams(vmem_limit_bytes=40 * 2**20),
    )(attended, w_output)


def solution(mesh):
    in_specs = (
        P("row", "col", None),
        P(),
        P(),
        P(),
        P(),
        P(),
        P("row", "col", None, None),
        P("row", "col", None, None),
    )
    return jax.shard_map(
        per_device, mesh=mesh, in_specs=in_specs, out_specs=P("row", "col", None), check_vma=False
    )
```

```python
import functools

import jax
import jax.numpy as jnp
from jax import lax
from jax.experimental import pallas as pl
from jax.experimental.pallas import tpu as pltpu
from jax.sharding import PartitionSpec as P

TILE = 8
LEVELS = 3
TOPK = 8
EPSILON = 1e-06
F32 = jnp.float32
BF16 = jnp.bfloat16
MESH = pl.DeviceIdType.MESH

DEVICES = 128
N_COL = 16
SIDE = 32
TOKENS = SIDE * SIDE
TILES = 16
REQUESTS = TILES * TOPK
WIDTH = 1024
HALF = WIDTH // 2
HEAD = 64
GROUP = 256
OWN = TILE * TILE
PER_LEVEL = TOPK * 4
KEYS = OWN + LEVELS * PER_LEVEL
N_ROW = 8
SERVED = 32


def wrap(value):
    return jnp.where(value >= 4, value - 4, value)


def row_shifted(place):
    row = lax.axis_index("row")
    y, core = lax.div(row, 2), lax.rem(row, 2)
    return wrap(y + place // 2) * 2 + (1 - core if place % 2 else core)


def col_shifted(place, sign):
    col = lax.axis_index("col")
    off_z = place % 4
    off_x = (place // 4 + 3 * off_z) % 4
    z = wrap(lax.div(col, 4) + (sign * off_z) % 4)
    x = wrap(lax.rem(col, 4) + (sign * off_x) % 4)
    return z * 4 + x


def iota(shape, axis):
    return lax.broadcasted_iota(jnp.int32, shape, axis)


def ones_where(condition):
    return jnp.where(condition, 1.0, 0.0)


def dot(a, b):
    return jnp.dot(a, b, preferred_element_type=F32)


def dot_rows(a, b):
    return lax.dot_general(a, b, (((1,), (1,)), ((), ())), preferred_element_type=F32)


def same_head():
    return ones_where(iota((GROUP, GROUP), 0) // HEAD == iota((GROUP, GROUP), 1) // HEAD).astype(BF16)


def unit_heads(values, block_ones):
    squares = values * values
    high = squares.astype(BF16)
    low = (squares - high.astype(F32)).astype(BF16)
    total = dot(high, block_ones) + dot(low, block_ones)
    return values * lax.rsqrt(total + EPSILON)


def column_of(raw_ref, level):
    raw = raw_ref[:, level].astype(F32).reshape(TILES, 1, TOPK)
    spread = jnp.broadcast_to(raw, (TILES, TOPK, TOPK))
    keep = iota((TILES, TOPK, TOPK), 1) == iota((TILES, TOPK, TOPK), 2)
    return jnp.sum(jnp.where(keep, spread, 0.0), axis=2, keepdims=True).reshape(REQUESTS, 1)


def row_of(column):
    square = (REQUESTS, REQUESTS)
    spread = jnp.broadcast_to(column, square)
    return jnp.sum(jnp.where(iota(square, 0) == iota(square, 1), spread, 0.0), axis=0, keepdims=True)


def kernel(
    tokens_hbm, gain_ref, w_query_hbm, w_keyval_hbm, scale_ref, parents_ref, counts_ref,
    attended,
    tokens, w_query, w_keyval, normed, queries, keys, values, marks, summed, weighed, picked,
    ask, passed, asked, send, recv, place_of,
    load_sem, pass_send, pass_recv, ask_send, ask_recv, reply_send, reply_recv, self_sem,
):
    square = (REQUESTS, REQUESTS)
    loads = [
        pltpu.make_async_copy(source, target, load_sem.at[number])
        for number, (source, target) in enumerate(
            ((tokens_hbm, tokens), (w_keyval_hbm, w_keyval), (w_query_hbm, w_query))
        )
    ]
    for load in loads:
        load.start()

    barrier = pltpu.get_barrier_semaphore()

    row, col = lax.axis_index("row"), lax.axis_index("col")
    me = row * N_COL + col

    rows_at = [row_shifted(place) for place in range(N_ROW)]
    cols_at = [col_shifted(place, 1) for place in range(N_COL)]
    for place in range(1, N_ROW):
        pl.semaphore_signal(barrier, inc=1, device_id=(rows_at[place], col), device_id_type=MESH)
    for place in range(1, N_COL):
        pl.semaphore_signal(barrier, inc=1, device_id=(row, cols_at[place]), device_id_type=MESH)

    lane = iota(square, 1)
    lane_level, lane_slot, lane_child = lane // 8, lane // 4 % 2, lane % 4
    table = jnp.zeros(square, F32)
    for level in range(LEVELS):
        parent_col = column_of(parents_ref, level).astype(jnp.int32)
        parent_row = row_of(parent_col.astype(F32)).astype(jnp.int32)
        bits = 8 - 2 * level
        home_col, home_row = parent_col >> bits, parent_row >> bits
        local_row = (parent_row & ((1 << bits) - 1)).astype(F32)
        same = home_col == home_row
        rank_col = jnp.sum(ones_where(same & (iota(square, 1) < iota(square, 0))), axis=1, keepdims=True)
        rank_row = jnp.sum(ones_where(same & (iota(square, 0) < iota(square, 1))), axis=0, keepdims=True)
        place_of[level] = jnp.broadcast_to(home_col * 8 + rank_col.astype(jnp.int32) * 4, square)
        for slot in range(2):
            here = (iota(square, 0) == home_row) & (rank_row == float(slot))
            cell = jnp.sum(jnp.where(here, local_row, 0.0), axis=1, keepdims=True)
            table = jnp.where((lane_level == level) & (lane_slot == slot), cell, table)
    local = table.astype(jnp.int32)
    wide_bits = 4 - lane_level
    parent_r, parent_c = local >> wide_bits, local & ((1 << wide_bits) - 1)
    child = ((2 * parent_r + lane_child // 2) << (wide_bits + 1)) + 2 * parent_c + lane_child % 2
    ask[...] = child.reshape(DEVICES, 1, REQUESTS)

    own_pass = pltpu.make_async_copy(ask.at[pl.ds(row * N_COL, N_COL)], passed.at[row], self_sem.at[LEVELS])
    own_pass.start()
    pl.semaphore_wait(barrier, N_ROW + N_COL - 2)

    for place in range(1, N_ROW):
        pltpu.make_async_remote_copy(
            src_ref=ask.at[pl.ds(rows_at[place] * N_COL, N_COL)], dst_ref=passed.at[row], send_sem=pass_send,
            recv_sem=pass_recv, device_id=(rows_at[place], col), device_id_type=MESH,
        ).start()

    loads[0].wait()
    gain = gain_ref[...].reshape(1, WIDTH)

    def norm_rows(pair, carry):
        flat = tokens[pl.ds(2 * pair, 2)].reshape(2 * SIDE, WIDTH).astype(F32)
        centered = flat - jnp.mean(flat, axis=1, keepdims=True)
        spread = jnp.mean(centered * centered, axis=1, keepdims=True)
        result = centered * lax.rsqrt(spread + EPSILON) * gain
        tiled = result.reshape(2, 4, TILE, WIDTH).transpose(1, 0, 2, 3).reshape(4, 16, WIDTH).astype(BF16)
        for tile in range(4):
            start = pl.multiple_of((pair // 4 * 4 + tile) * OWN + pair % 4 * 16, 16)
            normed[pl.ds(start, 16), :] = tiled[tile]
        return carry

    lax.fori_loop(0, SIDE // 4, norm_rows, 0)
    own_pass.wait()
    pltpu.make_async_remote_copy(
        src_ref=passed.at[pl.ds(0, N_ROW - 1)], dst_ref=passed.at[pl.ds(0, N_ROW - 1)], send_sem=pass_send,
        recv_sem=pass_recv, device_id=(rows_at[1], col), device_id_type=MESH,
    ).wait()
    own_ask = pltpu.make_async_copy(passed.at[:, col], asked.at[0], self_sem.at[LEVELS])
    own_ask.start()

    for place in range(1, N_COL):
        to = col_shifted(place, -1)
        pltpu.make_async_remote_copy(
            src_ref=passed.at[:, to], dst_ref=asked.at[place], send_sem=ask_send, recv_sem=ask_recv,
            device_id=(row, to), device_id_type=MESH,
        ).start()

    lax.fori_loop(SIDE // 4, SIDE // 2, norm_rows, 0)

    own_ask.wait()
    pltpu.make_async_remote_copy(
        src_ref=asked.at[pl.ds(0, N_COL - 1)], dst_ref=asked.at[pl.ds(0, N_COL - 1)], send_sem=ask_send,
        recv_sem=ask_recv, device_id=(row, cols_at[1]), device_id_type=MESH,
    ).wait()
    token = iota((1, TOKENS), 1)
    token_r = token // 256 * 8 + token // 8 % 8
    token_c = token // 64 % 4 * 8 + token % 8
    place_in_eight = iota((SERVED, 8, REQUESTS), 1)
    lane_in_eight = iota((SERVED, 8, REQUESTS), 2)

    def gather(levels, block):
        first = pl.multiple_of(block * SERVED, SERVED)
        asks = asked[pl.ds(block * 4, 4)].astype(F32).reshape(SERVED, 1, REQUESTS)
        asks = jnp.broadcast_to(asks, (SERVED, 8, REQUESTS))
        picks = []
        for level in levels:
            cell_of = (token_r >> level) * (SIDE >> level) + (token_c >> level)
            wanted = jnp.where(lane_in_eight == place_in_eight + 8 * level, asks, 0.0)
            wanted = jnp.sum(wanted, axis=2, keepdims=True).reshape(SERVED * 8, 1).astype(jnp.int32)
            picks.append(jnp.where(wanted == cell_of, 0.25**level, 0.0).astype(BF16))
        pick = jnp.concatenate(picks, axis=0)
        left = dot(pick, normed[:, :HALF]).reshape(len(levels), SERVED, 8, HALF)
        right = dot(pick, normed[:, HALF:]).reshape(len(levels), SERVED, 8, HALF)
        for number, level in enumerate(levels):
            both = jnp.concatenate([left[number], right[number]], axis=1)
            send[level, pl.ds(first, SERVED)] = both.astype(BF16)

    def send_replies(level, blocks):
        for turn in range(SERVED * len(blocks)):
            block, off_z = blocks[turn // SERVED], turn % 4
            place = (turn // 4 + off_z) % 4 * 2 + turn % SERVED // 16
            if block == 0 and off_z == 0 and place == 0:
                continue
            pltpu.make_async_remote_copy(
                src_ref=send.at[level, block * SERVED + off_z * N_ROW + rows_at[place]],
                dst_ref=recv.at[level, me], send_sem=reply_send.at[level], recv_sem=reply_recv.at[level],
                device_id=(rows_at[place], cols_at[block * 4 + off_z]), device_id_type=MESH,
            ).start()

    def all_replies(level):
        return pltpu.make_async_remote_copy(
            src_ref=send.at[level, pl.ds(0, DEVICES - 1)], dst_ref=recv.at[level, pl.ds(0, DEVICES - 1)],
            send_sem=reply_send.at[level], recv_sem=reply_recv.at[level],
            device_id=(rows_at[1], col), device_id_type=MESH,
        )

    def own_reply(level):
        return pltpu.make_async_copy(send.at[level, row], recv.at[level, me], self_sem.at[level])

    def gather_later(block, carry):
        gather((1, 2), block)
        return carry

    for block in range(DEVICES // SERVED):
        gather((0,), block)
        send_replies(0, (block,))
    lax.fori_loop(0, DEVICES // SERVED, gather_later, 0)
    send_replies(1, range(DEVICES // SERVED))
    for level in range(LEVELS):
        own_reply(level).start()

    block_ones = same_head()
    loads[1].wait()
    loads[2].wait()

    def project(block, carry):
        rows = pl.ds(pl.multiple_of(block * HALF, HALF), HALF)
        tiles = pl.ds(block * 8, 8)
        flat = normed[rows, :]
        for group in range(WIDTH // GROUP):
            span = slice(group * GROUP, (group + 1) * GROUP)
            scale = jnp.zeros((1, GROUP), F32)
            for head in range(4):
                scale = jnp.where(iota((1, GROUP), 1) // HEAD == head, scale_ref[group * 4 + head], scale)
            query = unit_heads(dot(flat, w_query[:, span]), block_ones) * scale
            queries[rows, span] = query.astype(BF16)
            key = dot(flat, w_keyval[:, span]).astype(BF16).astype(F32)
            keys[tiles, 0:OWN, span] = unit_heads(key, block_ones).astype(BF16).reshape(8, OWN, GROUP)
            value = dot(flat, w_keyval[:, WIDTH + group * GROUP : WIDTH + (group + 1) * GROUP])
            values[tiles, 0:OWN, span] = value.astype(BF16).reshape(8, OWN, GROUP)
        return carry

    lax.fori_loop(0, TOKENS // HALF, project, 0)
    marks[:, 0:OWN, :] = jnp.ones((TILES, OWN, REQUESTS), BF16)

    def by_tile(rows):
        columns = rows.shape[-1]
        return rows.reshape(4, TILES, TOPK, columns).transpose(1, 0, 2, 3).reshape(TILES, PER_LEVEL, columns)

    slots = iota((REQUESTS, DEVICES * 8), 1)
    early = OWN + PER_LEVEL

    def head_masks(count):
        return [ones_where(iota((count, GROUP), 1) // HEAD == head).astype(BF16) for head in range(4)]

    def marks_over(tile, first, last):
        mark = marks[tile, first:last]
        mark = jnp.concatenate([mark, mark], axis=1)
        return jnp.concatenate([mark * mask for mask in head_masks(last - first)], axis=0)

    def sums_over(tile, group, mark, first, last):
        masks = head_masks(last - first)
        rows = pl.ds(pl.multiple_of(tile * OWN, OWN), OWN)
        span = slice(group * GROUP, (group + 1) * GROUP)
        key = jnp.concatenate([keys[tile, first:last, span] * mask for mask in masks], axis=0)
        value = jnp.concatenate([values[tile, first:last, span] * mask for mask in masks], axis=0)
        weight = jnp.exp(dot_rows(queries[rows, span], key)).astype(BF16)
        return rows, span, dot(weight, value), dot(weight, mark)

    def early_keys(tile, carry):
        mark = marks_over(tile, 0, early)
        for group in range(WIDTH // GROUP):
            rows, span, top, bottom = sums_over(tile, group, mark, 0, early)
            summed[rows, span] = top
            weighed[rows, span] = bottom
        return carry

    send_replies(2, range(DEVICES // SERVED))
    for level in range(LEVELS):
        if level == 1:
            lax.fori_loop(0, TILES, early_keys, 0, unroll=2)
        own_reply(level).wait()
        all_replies(level).wait()
        count_col = column_of(counts_ref, level)
        place_col = place_of[level][:, 0:1]
        valid = [count_col > float(child) for child in range(4)]
        marks[:, OWN + level * PER_LEVEL : OWN + (level + 1) * PER_LEVEL, :] = by_tile(
            jnp.concatenate([jnp.broadcast_to(ones_where(flag), square) for flag in valid], axis=0)
        ).astype(BF16)
        pick = jnp.concatenate(
            [ones_where((slots == place_col + child) & valid[child]).astype(BF16) for child in range(4)], axis=0
        )
        for side in range(2):
            rows = recv[level].astype(F32)[:, side * 8 : side * 8 + 8, :].reshape(DEVICES * 8, HALF).astype(BF16)
            picked[:, side * HALF : (side + 1) * HALF] = dot(pick, rows).astype(BF16)
        span_rows = slice(OWN + level * PER_LEVEL, OWN + (level + 1) * PER_LEVEL)
        for group in range(WIDTH // GROUP):
            span = slice(group * GROUP, (group + 1) * GROUP)
            key = dot(picked[...], w_keyval[:, span]).astype(BF16).astype(F32)
            keys[:, span_rows, span] = by_tile(unit_heads(key, block_ones)).astype(BF16)
            value = dot(picked[...], w_keyval[:, WIDTH + group * GROUP : WIDTH + (group + 1) * GROUP])
            values[:, span_rows, span] = by_tile(value).astype(BF16)

    def last_keys(tile, carry):
        mark = marks_over(tile, early, KEYS)
        for group in range(WIDTH // GROUP):
            rows, span, top, bottom = sums_over(tile, group, mark, early, KEYS)
            attended[rows, span] = ((summed[rows, span] + top) / (weighed[rows, span] + bottom)).astype(BF16)
        return carry

    lax.fori_loop(0, TILES, last_keys, 0, unroll=4)


def mix(attended, w_output, out_hbm, mixed, store_sem):
    blocks = TILES // 4
    stores = [
        pltpu.make_async_copy(
            mixed.at[pl.ds(block * TILE, TILE)], out_hbm.at[pl.ds(block * TILE, TILE)], store_sem.at[block]
        )
        for block in range(blocks)
    ]
    for block in range(blocks):
        result = dot(attended[block * GROUP : (block + 1) * GROUP], w_output[...]).reshape(4, TILE, TILE, WIDTH)
        result = result.transpose(1, 0, 2, 3).reshape(TILE, SIDE, WIDTH)
        mixed[block * TILE : (block + 1) * TILE] = result.astype(BF16)
        stores[block].start()
    for store in stores:
        store.wait()


def per_device(tokens, ln_gain, w_query, w_keyval, logit_scale, w_output, parents, child_counts):
    whole = pl.BlockSpec(memory_space=pltpu.VMEM)
    anywhere = pl.BlockSpec(memory_space=pl.ANY)
    attended = pl.pallas_call(
        kernel,
        out_shape=jax.ShapeDtypeStruct((TOKENS, WIDTH), BF16),
        in_specs=[anywhere, whole, anywhere, anywhere, pl.BlockSpec(memory_space=pltpu.SMEM), whole, whole],
        out_specs=whole,
        scratch_shapes=[
            pltpu.VMEM((SIDE, SIDE, WIDTH), BF16),
            pltpu.VMEM((WIDTH, WIDTH), BF16),
            pltpu.VMEM((WIDTH, 2 * WIDTH), BF16),
            pltpu.VMEM((TOKENS, WIDTH), BF16),
            pltpu.VMEM((TOKENS, WIDTH), BF16),
            pltpu.VMEM((TILES, KEYS, WIDTH), BF16),
            pltpu.VMEM((TILES, KEYS, WIDTH), BF16),
            pltpu.VMEM((TILES, KEYS, REQUESTS), BF16),
            pltpu.VMEM((TOKENS, WIDTH), F32),
            pltpu.VMEM((TOKENS, WIDTH), F32),
            pltpu.VMEM((4 * REQUESTS, WIDTH), BF16),
            pltpu.VMEM((DEVICES, 1, REQUESTS), jnp.int32),
            pltpu.VMEM((N_ROW, N_COL, 1, REQUESTS), jnp.int32),
            pltpu.VMEM((N_COL, N_ROW, 1, REQUESTS), jnp.int32),
            pltpu.VMEM((LEVELS, DEVICES, 16, HALF), BF16),
            pltpu.VMEM((LEVELS, DEVICES, 16, HALF), BF16),
            pltpu.VMEM((LEVELS, REQUESTS, REQUESTS), jnp.int32),
            pltpu.SemaphoreType.DMA((3,)),
            pltpu.SemaphoreType.DMA,
            pltpu.SemaphoreType.DMA,
            pltpu.SemaphoreType.DMA,
            pltpu.SemaphoreType.DMA,
            pltpu.SemaphoreType.DMA((LEVELS,)),
            pltpu.SemaphoreType.DMA((LEVELS,)),
            pltpu.SemaphoreType.DMA((LEVELS + 1,)),
        ],
        compiler_params=pltpu.CompilerParams(
            collective_id=0, has_side_effects=True, vmem_limit_bytes=60 * 2**20
        ),
    )(tokens, ln_gain, w_query, w_keyval, logit_scale, parents.transpose(0, 2, 1, 3), child_counts.transpose(0, 2, 1, 3))
    return pl.pallas_call(
        mix,
        out_shape=jax.ShapeDtypeStruct((SIDE, SIDE, WIDTH), BF16),
        in_specs=[whole, whole],
        out_specs=pl.BlockSpec(memory_space=pltpu.HBM),
        scratch_shapes=[
            pltpu.VMEM((SIDE, SIDE, WIDTH), BF16),
            pltpu.SemaphoreType.DMA((TILES // 4,)),
        ],
        compiler_params=pltpu.CompilerParams(vmem_limit_bytes=24 * 2**20),
    )(attended, w_output)


def solution(mesh):
    in_specs = (
        P("row", "col", None),
        P(),
        P(),
        P(),
        P(),
        P(),
        P("row", "col", None, None),
        P("row", "col", None, None),
    )
    return jax.shard_map(
        per_device, mesh=mesh, in_specs=in_specs, out_specs=P("row", "col", None), check_vma=False
    )
```

```python
import functools

import jax
import jax.numpy as jnp
from jax import lax
from jax.experimental import pallas as pl
from jax.experimental.pallas import tpu as pltpu
from jax.sharding import PartitionSpec as P

TILE = 8
LEVELS = 3
TOPK = 8
EPSILON = 1e-06
F32 = jnp.float32
BF16 = jnp.bfloat16
MESH = pl.DeviceIdType.MESH

DEVICES = 128
N_COL = 16
SIDE = 32
TOKENS = SIDE * SIDE
TILES = 16
REQUESTS = TILES * TOPK
WIDTH = 1024
HALF = WIDTH // 2
HEAD = 64
GROUP = 256
OWN = TILE * TILE
PER_LEVEL = TOPK * 4
KEYS = OWN + LEVELS * PER_LEVEL
N_ROW = 8
SERVED = 32


def wrap(value):
    return jnp.where(value >= 4, value - 4, value)


def row_shifted(place):
    row = lax.axis_index("row")
    y, core = lax.div(row, 2), lax.rem(row, 2)
    return wrap(y + place // 2) * 2 + (1 - core if place % 2 else core)


def col_shifted(place, sign):
    col = lax.axis_index("col")
    off_z = place % 4
    off_x = (place // 4 + 3 * off_z) % 4
    z = wrap(lax.div(col, 4) + (sign * off_z) % 4)
    x = wrap(lax.rem(col, 4) + (sign * off_x) % 4)
    return z * 4 + x


def iota(shape, axis):
    return lax.broadcasted_iota(jnp.int32, shape, axis)


def ones_where(condition):
    return jnp.where(condition, 1.0, 0.0)


def dot(a, b):
    return jnp.dot(a, b, preferred_element_type=F32)


def dot_rows(a, b):
    return lax.dot_general(a, b, (((1,), (1,)), ((), ())), preferred_element_type=F32)


def same_head():
    return ones_where(iota((GROUP, GROUP), 0) // HEAD == iota((GROUP, GROUP), 1) // HEAD).astype(BF16)


def unit_heads(values, block_ones):
    squares = values * values
    high = squares.astype(BF16)
    low = (squares - high.astype(F32)).astype(BF16)
    total = dot(high, block_ones) + dot(low, block_ones)
    return values * lax.rsqrt(total + EPSILON)


def column_of(raw_ref, level):
    raw = raw_ref[:, level].astype(F32).reshape(TILES, 1, TOPK)
    spread = jnp.broadcast_to(raw, (TILES, TOPK, TOPK))
    keep = iota((TILES, TOPK, TOPK), 1) == iota((TILES, TOPK, TOPK), 2)
    return jnp.sum(jnp.where(keep, spread, 0.0), axis=2, keepdims=True).reshape(REQUESTS, 1)


def row_of(column):
    square = (REQUESTS, REQUESTS)
    spread = jnp.broadcast_to(column, square)
    return jnp.sum(jnp.where(iota(square, 0) == iota(square, 1), spread, 0.0), axis=0, keepdims=True)


def kernel(
    tokens_hbm, gain_ref, w_query_hbm, w_keyval_hbm, scale_ref, parents_ref, counts_ref,
    attended,
    tokens, w_query, w_keyval, normed, queries, keys, values, marks, summed, weighed, picked,
    ask, passed, asked, send, recv, place_of,
    load_sem, pass_send, pass_recv, ask_send, ask_recv, reply_send, reply_recv, self_sem,
):
    square = (REQUESTS, REQUESTS)
    loads = [
        pltpu.make_async_copy(source, target, load_sem.at[number])
        for number, (source, target) in enumerate(
            ((tokens_hbm, tokens), (w_keyval_hbm, w_keyval), (w_query_hbm, w_query))
        )
    ]
    for load in loads:
        load.start()

    barrier = pltpu.get_barrier_semaphore()

    row, col = lax.axis_index("row"), lax.axis_index("col")
    me = row * N_COL + col

    rows_at = [row_shifted(place) for place in range(N_ROW)]
    cols_at = [col_shifted(place, 1) for place in range(N_COL)]
    for place in range(1, N_ROW):
        pl.semaphore_signal(barrier, inc=1, device_id=(rows_at[place], col), device_id_type=MESH)
    for place in range(1, N_COL):
        pl.semaphore_signal(barrier, inc=1, device_id=(row, cols_at[place]), device_id_type=MESH)

    lane = iota(square, 1)
    lane_level, lane_slot, lane_child = lane // 8, lane // 4 % 2, lane % 4
    table = jnp.zeros(square, F32)
    for level in range(LEVELS):
        parent_col = column_of(parents_ref, level).astype(jnp.int32)
        parent_row = row_of(parent_col.astype(F32)).astype(jnp.int32)
        bits = 8 - 2 * level
        home_col, home_row = parent_col >> bits, parent_row >> bits
        local_row = (parent_row & ((1 << bits) - 1)).astype(F32)
        same = home_col == home_row
        rank_col = jnp.sum(ones_where(same & (iota(square, 1) < iota(square, 0))), axis=1, keepdims=True)
        rank_row = jnp.sum(ones_where(same & (iota(square, 0) < iota(square, 1))), axis=0, keepdims=True)
        place_of[level] = jnp.broadcast_to(home_col * 8 + rank_col.astype(jnp.int32) * 4, square)
        for slot in range(2):
            here = (iota(square, 0) == home_row) & (rank_row == float(slot))
            cell = jnp.sum(jnp.where(here, local_row, 0.0), axis=1, keepdims=True)
            table = jnp.where((lane_level == level) & (lane_slot == slot), cell, table)
    local = table.astype(jnp.int32)
    wide_bits = 4 - lane_level
    parent_r, parent_c = local >> wide_bits, local & ((1 << wide_bits) - 1)
    child = ((2 * parent_r + lane_child // 2) << (wide_bits + 1)) + 2 * parent_c + lane_child % 2
    ask[...] = child.reshape(DEVICES, 1, REQUESTS)

    own_pass = pltpu.make_async_copy(ask.at[pl.ds(row * N_COL, N_COL)], passed.at[row], self_sem.at[LEVELS])
    own_pass.start()
    pl.semaphore_wait(barrier, N_ROW + N_COL - 2)

    for place in range(1, N_ROW):
        pltpu.make_async_remote_copy(
            src_ref=ask.at[pl.ds(rows_at[place] * N_COL, N_COL)], dst_ref=passed.at[row], send_sem=pass_send,
            recv_sem=pass_recv, device_id=(rows_at[place], col), device_id_type=MESH,
        ).start()

    loads[0].wait()
    gain = gain_ref[...].reshape(1, WIDTH)

    def norm_rows(pair, carry):
        flat = tokens[pl.ds(2 * pair, 2)].reshape(2 * SIDE, WIDTH).astype(F32)
        centered = flat - jnp.mean(flat, axis=1, keepdims=True)
        spread = jnp.mean(centered * centered, axis=1, keepdims=True)
        result = centered * lax.rsqrt(spread + EPSILON) * gain
        tiled = result.reshape(2, 4, TILE, WIDTH).transpose(1, 0, 2, 3).reshape(4, 16, WIDTH).astype(BF16)
        for tile in range(4):
            start = pl.multiple_of((pair // 4 * 4 + tile) * OWN + pair % 4 * 16, 16)
            normed[pl.ds(start, 16), :] = tiled[tile]
        return carry

    lax.fori_loop(0, SIDE // 4, norm_rows, 0)
    own_pass.wait()
    pltpu.make_async_remote_copy(
        src_ref=passed.at[pl.ds(0, N_ROW - 1)], dst_ref=passed.at[pl.ds(0, N_ROW - 1)], send_sem=pass_send,
        recv_sem=pass_recv, device_id=(rows_at[1], col), device_id_type=MESH,
    ).wait()
    own_ask = pltpu.make_async_copy(passed.at[:, col], asked.at[0], self_sem.at[LEVELS])
    own_ask.start()

    for place in range(1, N_COL):
        to = col_shifted(place, -1)
        pltpu.make_async_remote_copy(
            src_ref=passed.at[:, to], dst_ref=asked.at[place], send_sem=ask_send, recv_sem=ask_recv,
            device_id=(row, to), device_id_type=MESH,
        ).start()

    lax.fori_loop(SIDE // 4, SIDE // 2, norm_rows, 0)

    own_ask.wait()
    pltpu.make_async_remote_copy(
        src_ref=asked.at[pl.ds(0, N_COL - 1)], dst_ref=asked.at[pl.ds(0, N_COL - 1)], send_sem=ask_send,
        recv_sem=ask_recv, device_id=(row, cols_at[1]), device_id_type=MESH,
    ).wait()
    token = iota((1, TOKENS), 1)
    token_r = token // 256 * 8 + token // 8 % 8
    token_c = token // 64 % 4 * 8 + token % 8
    place_in_eight = iota((SERVED, 8, REQUESTS), 1)
    lane_in_eight = iota((SERVED, 8, REQUESTS), 2)

    def gather(levels, block):
        first = pl.multiple_of(block * SERVED, SERVED)
        asks = asked[pl.ds(block * 4, 4)].astype(F32).reshape(SERVED, 1, REQUESTS)
        asks = jnp.broadcast_to(asks, (SERVED, 8, REQUESTS))
        picks = []
        for level in levels:
            cell_of = (token_r >> level) * (SIDE >> level) + (token_c >> level)
            wanted = jnp.where(lane_in_eight == place_in_eight + 8 * level, asks, 0.0)
            wanted = jnp.sum(wanted, axis=2, keepdims=True).reshape(SERVED * 8, 1).astype(jnp.int32)
            picks.append(jnp.where(wanted == cell_of, 0.25**level, 0.0).astype(BF16))
        pick = jnp.concatenate(picks, axis=0)
        left = dot(pick, normed[:, :HALF]).reshape(len(levels), SERVED, 8, HALF)
        right = dot(pick, normed[:, HALF:]).reshape(len(levels), SERVED, 8, HALF)
        for number, level in enumerate(levels):
            both = jnp.concatenate([left[number], right[number]], axis=1)
            send[level, pl.ds(first, SERVED)] = both.astype(BF16)

    def send_replies(level, blocks):
        for turn in range(SERVED * len(blocks)):
            block, off_z = blocks[turn // SERVED], turn % 4
            place = (turn // 4 + off_z) % 4 * 2 + turn % SERVED // 16
            if block == 0 and off_z == 0 and place == 0:
                continue
            pltpu.make_async_remote_copy(
                src_ref=send.at[level, block * SERVED + off_z * N_ROW + rows_at[place]],
                dst_ref=recv.at[level, me], send_sem=reply_send.at[level], recv_sem=reply_recv.at[level],
                device_id=(rows_at[place], cols_at[block * 4 + off_z]), device_id_type=MESH,
            ).start()

    def all_replies(level):
        return pltpu.make_async_remote_copy(
            src_ref=send.at[level, pl.ds(0, DEVICES - 1)], dst_ref=recv.at[level, pl.ds(0, DEVICES - 1)],
            send_sem=reply_send.at[level], recv_sem=reply_recv.at[level],
            device_id=(rows_at[1], col), device_id_type=MESH,
        )

    def own_reply(level):
        return pltpu.make_async_copy(send.at[level, row], recv.at[level, me], self_sem.at[level])

    def gather_later(block, carry):
        gather((1, 2), block)
        return carry

    for block in range(DEVICES // SERVED):
        gather((0,), block)
        send_replies(0, (block,))
    lax.fori_loop(0, DEVICES // SERVED, gather_later, 0)
    send_replies(1, range(DEVICES // SERVED))
    for level in range(LEVELS):
        own_reply(level).start()

    block_ones = same_head()
    loads[1].wait()
    loads[2].wait()

    def project(block, carry):
        rows = pl.ds(pl.multiple_of(block * HALF, HALF), HALF)
        tiles = pl.ds(block * 8, 8)
        flat = normed[rows, :]
        for group in range(WIDTH // GROUP):
            span = slice(group * GROUP, (group + 1) * GROUP)
            scale = jnp.zeros((1, GROUP), F32)
            for head in range(4):
                scale = jnp.where(iota((1, GROUP), 1) // HEAD == head, scale_ref[group * 4 + head], scale)
            query = unit_heads(dot(flat, w_query[:, span]), block_ones) * scale
            queries[rows, span] = query.astype(BF16)
            key = dot(flat, w_keyval[:, span]).astype(BF16).astype(F32)
            keys[tiles, 0:OWN, span] = unit_heads(key, block_ones).astype(BF16).reshape(8, OWN, GROUP)
            value = dot(flat, w_keyval[:, WIDTH + group * GROUP : WIDTH + (group + 1) * GROUP])
            values[tiles, 0:OWN, span] = value.astype(BF16).reshape(8, OWN, GROUP)
        return carry

    lax.fori_loop(0, TOKENS // HALF, project, 0)
    marks[:, 0:OWN, :] = jnp.ones((TILES, OWN, REQUESTS), BF16)

    def by_tile(rows):
        columns = rows.shape[-1]
        return rows.reshape(4, TILES, TOPK, columns).transpose(1, 0, 2, 3).reshape(TILES, PER_LEVEL, columns)

    slots = iota((REQUESTS, DEVICES * 8), 1)
    early = OWN + PER_LEVEL

    def head_masks(count):
        return [ones_where(iota((count, GROUP), 1) // HEAD == head).astype(BF16) for head in range(4)]

    def marks_over(tile, first, last):
        mark = marks[tile, first:last]
        mark = jnp.concatenate([mark, mark], axis=1)
        return jnp.concatenate([mark * mask for mask in head_masks(last - first)], axis=0)

    def sums_over(tile, first, last):
        masks = head_masks(last - first)
        rows = pl.ds(pl.multiple_of(tile * OWN, OWN), OWN)
        weights, tops = [], []
        for group in range(WIDTH // GROUP):
            span = slice(group * GROUP, (group + 1) * GROUP)
            key = jnp.concatenate([keys[tile, first:last, span] * mask for mask in masks], axis=0)
            value = jnp.concatenate([values[tile, first:last, span] * mask for mask in masks], axis=0)
            weights.append(jnp.exp(dot_rows(queries[rows, span], key)).astype(BF16))
            tops.append(dot(weights[group], value))
        bottoms = dot(jnp.concatenate(weights, axis=0), marks_over(tile, first, last))
        for group in range(WIDTH // GROUP):
            span = slice(group * GROUP, (group + 1) * GROUP)
            yield rows, span, tops[group], bottoms[group * OWN : (group + 1) * OWN]

    def early_keys(tile, carry):
        for rows, span, top, bottom in sums_over(tile, 0, early):
            summed[rows, span] = top
            weighed[rows, span] = bottom
        return carry

    send_replies(2, range(DEVICES // SERVED))
    for level in range(LEVELS):
        if level == 1:
            lax.fori_loop(0, TILES, early_keys, 0, unroll=2)
        own_reply(level).wait()
        all_replies(level).wait()
        count_col = column_of(counts_ref, level)
        place_col = place_of[level][:, 0:1]
        valid = [count_col > float(child) for child in range(4)]
        marks[:, OWN + level * PER_LEVEL : OWN + (level + 1) * PER_LEVEL, :] = by_tile(
            jnp.concatenate([jnp.broadcast_to(ones_where(flag), square) for flag in valid], axis=0)
        ).astype(BF16)
        pick = jnp.concatenate(
            [ones_where((slots == place_col + child) & valid[child]).astype(BF16) for child in range(4)], axis=0
        )
        for side in range(2):
            rows = recv[level].astype(F32)[:, side * 8 : side * 8 + 8, :].reshape(DEVICES * 8, HALF).astype(BF16)
            picked[:, side * HALF : (side + 1) * HALF] = dot(pick, rows).astype(BF16)
        span_rows = slice(OWN + level * PER_LEVEL, OWN + (level + 1) * PER_LEVEL)
        for group in range(WIDTH // GROUP):
            span = slice(group * GROUP, (group + 1) * GROUP)
            key = dot(picked[...], w_keyval[:, span]).astype(BF16).astype(F32)
            keys[:, span_rows, span] = by_tile(unit_heads(key, block_ones)).astype(BF16)
            value = dot(picked[...], w_keyval[:, WIDTH + group * GROUP : WIDTH + (group + 1) * GROUP])
            values[:, span_rows, span] = by_tile(value).astype(BF16)

    def last_keys(tile, carry):
        for rows, span, top, bottom in sums_over(tile, early, KEYS):
            attended[rows, span] = ((summed[rows, span] + top) / (weighed[rows, span] + bottom)).astype(BF16)
        return carry

    lax.fori_loop(0, TILES, last_keys, 0, unroll=4)


def mix(attended, w_output, out_hbm, mixed, store_sem):
    blocks = TILES // 4
    stores = [
        pltpu.make_async_copy(
            mixed.at[pl.ds(block * TILE, TILE)], out_hbm.at[pl.ds(block * TILE, TILE)], store_sem.at[block]
        )
        for block in range(blocks)
    ]
    for block in range(blocks):
        result = dot(attended[block * GROUP : (block + 1) * GROUP], w_output[...]).reshape(4, TILE, TILE, WIDTH)
        result = result.transpose(1, 0, 2, 3).reshape(TILE, SIDE, WIDTH)
        mixed[block * TILE : (block + 1) * TILE] = result.astype(BF16)
        stores[block].start()
    for store in stores:
        store.wait()


def per_device(tokens, ln_gain, w_query, w_keyval, logit_scale, w_output, parents, child_counts):
    whole = pl.BlockSpec(memory_space=pltpu.VMEM)
    anywhere = pl.BlockSpec(memory_space=pl.ANY)
    attended = pl.pallas_call(
        kernel,
        out_shape=jax.ShapeDtypeStruct((TOKENS, WIDTH), BF16),
        in_specs=[anywhere, whole, anywhere, anywhere, pl.BlockSpec(memory_space=pltpu.SMEM), whole, whole],
        out_specs=whole,
        scratch_shapes=[
            pltpu.VMEM((SIDE, SIDE, WIDTH), BF16),
            pltpu.VMEM((WIDTH, WIDTH), BF16),
            pltpu.VMEM((WIDTH, 2 * WIDTH), BF16),
            pltpu.VMEM((TOKENS, WIDTH), BF16),
            pltpu.VMEM((TOKENS, WIDTH), BF16),
            pltpu.VMEM((TILES, KEYS, WIDTH), BF16),
            pltpu.VMEM((TILES, KEYS, WIDTH), BF16),
            pltpu.VMEM((TILES, KEYS, REQUESTS), BF16),
            pltpu.VMEM((TOKENS, WIDTH), F32),
            pltpu.VMEM((TOKENS, WIDTH), F32),
            pltpu.VMEM((4 * REQUESTS, WIDTH), BF16),
            pltpu.VMEM((DEVICES, 1, REQUESTS), jnp.int32),
            pltpu.VMEM((N_ROW, N_COL, 1, REQUESTS), jnp.int32),
            pltpu.VMEM((N_COL, N_ROW, 1, REQUESTS), jnp.int32),
            pltpu.VMEM((LEVELS, DEVICES, 16, HALF), BF16),
            pltpu.VMEM((LEVELS, DEVICES, 16, HALF), BF16),
            pltpu.VMEM((LEVELS, REQUESTS, REQUESTS), jnp.int32),
            pltpu.SemaphoreType.DMA((3,)),
            pltpu.SemaphoreType.DMA,
            pltpu.SemaphoreType.DMA,
            pltpu.SemaphoreType.DMA,
            pltpu.SemaphoreType.DMA,
            pltpu.SemaphoreType.DMA((LEVELS,)),
            pltpu.SemaphoreType.DMA((LEVELS,)),
            pltpu.SemaphoreType.DMA((LEVELS + 1,)),
        ],
        compiler_params=pltpu.CompilerParams(
            collective_id=0, has_side_effects=True, vmem_limit_bytes=60 * 2**20
        ),
    )(tokens, ln_gain, w_query, w_keyval, logit_scale, parents.transpose(0, 2, 1, 3), child_counts.transpose(0, 2, 1, 3))
    return pl.pallas_call(
        mix,
        out_shape=jax.ShapeDtypeStruct((SIDE, SIDE, WIDTH), BF16),
        in_specs=[whole, whole],
        out_specs=pl.BlockSpec(memory_space=pltpu.HBM),
        scratch_shapes=[
            pltpu.VMEM((SIDE, SIDE, WIDTH), BF16),
            pltpu.SemaphoreType.DMA((TILES // 4,)),
        ],
        compiler_params=pltpu.CompilerParams(vmem_limit_bytes=24 * 2**20),
    )(attended, w_output)


def solution(mesh):
    in_specs = (
        P("row", "col", None),
        P(),
        P(),
        P(),
        P(),
        P(),
        P("row", "col", None, None),
        P("row", "col", None, None),
    )
    return jax.shard_map(
        per_device, mesh=mesh, in_specs=in_specs, out_specs=P("row", "col", None), check_vma=False
    )
```
